32 devices in a mesh: dp: 2 (over y), section: 4 (over x, core), head: 4 (over z).
Axes of the slice: x: 2, y: 2, z: 4, core: 2. Of those that a mesh axis runs over, the one named last changes fastest.
Arguments:
- images: bfloat16 [8, 144, 1408], P(('dp', 'head')), may hold values from -6 to 6
- w_in: bfloat16 [4, 1408, 3072], P('section'), may hold values from -0.15625 to 0.15625
- w_out: bfloat16 [4, 3072, 1408], P('section'), may hold values from -0.109375 to 0.109375
- fpn_weight: bfloat16 [2, 1408, 256], P(None, None, 'section'), may hold values from -0.15625 to 0.15625
- fc6_weight: bfloat16 [256, 49, 512], P('section'), may hold values from -0.0546875 to 0.0546875
- fc7_weight: bfloat16 [512, 512], replicated, may hold values from -0.25 to 0.25
- windows: int32 [3, 8, 128], P(None, ('dp', 'head')), may hold values from 0 to 8, as said below
- bilinear: float32 [2, 7, 4, 8, 128], P(None, None, None, ('dp', 'head')), may hold values from 0 to 1, as said below
- owners: int32 [8, 128, 1], P(('dp', 'head')), may hold values from 0 to 7; in each aligned block of 128 rows (0 to 127, 128 to 255, ..., all dimensions but the last counted through in order) at most 24 rows name the same one
- cotangent: bfloat16 [8, 8, 24, 512], P(('dp', 'head')), may hold values from -6 to 6
Outputs:
- grad_w_in: float32 [4, 1408, 3072], P('section', ('dp', 'head'))
- grad_w_out: float32 [4, 3072, 1408], P('section', ('dp', 'head'))
- grad_fpn: float32 [2, 1408, 256], P(None, None, 'section')
- grad_fc6: float32 [256, 49, 512], P('section', None, ('dp', 'head'))
- grad_fc7: float32 [512, 512], P(None, ('dp', 'head'))
The draws below stay inside these ranges and needn't reach their ends.
Inputs may be any that keep to these rules, and one draw needn't show every extreme that they name: windows[0] is the level (0 or 1); windows[1] and windows[2] are a corner such that a 4x4 window fits the level's grid (12 or 6 cells a side). Along u each row of bilinear has at most two nonzero weights, on adjacent cells, summing to one. `owners`: among the 128 boxes of one image group (aligned blocks) no owner is named more than 24 times.
All inputs are finite; a program needn't handle non-finite values.
Results may differ from the reference program's by a relative error of at most 0.035.
Values may be sent and summed in bfloat16 or wider, within the bound.
A program may use at most 128 MiB of HBM per device.

```python
import math
import jax
import jax.numpy as jnp
import numpy as np
from jax import lax

D = 1408
FFW = 3072
CHANNELS = 256
HEAD_UNITS = 512
GRID = 12
SPAN = 4
POOLED = 7
IMG_DEV = 1
BOX_IMG = 128
LAYERS = 4
OWNERS = 8
IMAGES = 8
CAP = 24
N_DP = 2
N_HEAD = 4


def draw_windows(key, part):
    key_level, key_corner = jax.random.split(key)
    levels = jax.random.randint(key_level, (IMAGES, BOX_IMG), 0, 2, dtype=jnp.int32)
    corner_pos = jax.random.randint(key_corner, (2, IMAGES, BOX_IMG), 0, GRID - SPAN + 1, dtype=jnp.int32)
    narrow = GRID // 2 - SPAN + 1
    anchors = jnp.where(levels[None] == 0, corner_pos, corner_pos % narrow)
    return jnp.concatenate([levels[None], anchors], axis=0).astype(jnp.int32)


def draw_bilinear(key, part):
    key_cell, key_frac = jax.random.split(key)
    lower_cell = jax.random.randint(key_cell, (2, POOLED, 1, IMAGES, BOX_IMG), 0, SPAN - 1, dtype=jnp.int32)
    fraction = jax.random.uniform(key_frac, (2, POOLED, 1, IMAGES, BOX_IMG), jnp.float32)
    cell_ids = jnp.arange(SPAN, dtype=jnp.int32).reshape(1, 1, SPAN, 1, 1)
    low_part = (1.0 - fraction) * (cell_ids == lower_cell).astype(jnp.float32)
    high_part = fraction * (cell_ids == lower_cell + 1).astype(jnp.float32)
    return (low_part + high_part).astype(jnp.float32)


def steps_of(stream_key, extent, cuts, least, largest):
    factor_of = 1.0
    for dim, shards_of in cuts:
        heights = jax.random.uniform(jax.random.fold_in(jax.random.fold_in(stream_key, 6), dim), (shards_of,), jnp.float32, least / len(cuts), largest / len(cuts))
        factor_of = factor_of * jnp.repeat(jnp.exp(heights), extent[dim] // shards_of).reshape((-1,) + (1,) * (len(extent) - 1 - dim))
    return factor_of


def routed_block(rng, own, number, rows, number_of, top, reach, lean):
    order = jax.random.permutation(rng, number_of)
    crowded, ordinary = shares(number_of, rows * top, reach, lean, True), shares(number_of, rows * top, reach, lean, False)
    places = jnp.arange(number_of)

    def named(sizes, rotation):
        used = int((sizes > 0).sum())
        fixed = max(1, used // 4)
        passed = fixed + (places - fixed + rotation * (used - fixed)) % max(1, number_of - fixed)
        return jnp.zeros((number_of,), jnp.int32).at[order[jnp.where(places < fixed, places, passed)]].set(jnp.asarray(sizes, jnp.int32))

    sizes = jnp.where(number % 4 == 0, named(crowded, number // 4), named(ordinary, number - number // 4 - 1))
    mixed = jax.random.permutation(jax.random.fold_in(own, 3), number_of)
    source_of, taker = mixed[0:number_of // 2 * 2:2], mixed[1:number_of // 2 * 2:2]
    slack = jnp.minimum(sizes[source_of] - 1, reach - sizes[taker]) // 2
    slack = jnp.where((source_of == order[0]) | (taker == order[0]) | (sizes[taker] == 0), 0, jnp.maximum(slack, 0))
    passed = jax.random.randint(jax.random.fold_in(own, 4), (number_of // 2,), 0, 1 << 20) % (slack + 1)
    sizes = sizes.at[source_of].add(-passed).at[taker].add(passed)
    labels = jnp.searchsorted(jnp.cumsum(sizes), jnp.arange(rows * top), side="right").astype(jnp.int32)
    table = labels.reshape(top, rows).T
    table = table[jax.random.permutation(jax.random.fold_in(own, 1), rows)]
    rotation = jax.random.randint(jax.random.fold_in(own, 2), (rows, 1), 0, top)
    return jnp.take_along_axis(table, (jnp.arange(top)[None, :] + rotation) % top, axis=1)


def shares(amount, total, bound, lean, full):
    loads = [(1 << 20) // math.isqrt(standing ** lean) + 1 for standing in range(1, amount + 1)]
    largest = bound if full else min(bound, max(-(-total // amount), total * loads[0] // sum(loads)))
    least = 1 if total - largest >= amount - 1 else 0
    counts, rest = [largest] + [least] * (amount - 1), total - largest - least * (amount - 1)
    while rest > 0:
        movable = [i for i in range(1, amount) if counts[i] < largest] or [i for i in range(1, amount) if counts[i] < bound]
        pool, budget = sum([loads[i] for i in movable]), rest
        for i in movable:
            extra = min(bound - counts[i], max(1, budget * loads[i] // pool), rest)
            counts[i] = counts[i] + extra
            rest = rest - extra
    return np.array(counts)


def gaussian(key, shape, spread, limit, cuts=(), held_as=jnp.bfloat16):
    factor_of = steps_of(key, shape, cuts, -0.22, 0.18) if cuts else 1.0
    entries = jax.random.normal(key, shape, jnp.float32) * spread * factor_of
    return jnp.minimum(jnp.maximum(entries, -limit), limit).astype(held_as)


def setup_inputs(seed: int = 0) -> dict:
    key_of = jax.random.split(jax.random.key(seed), 11)
    images = gaussian(key_of[0], (IMAGES, GRID * GRID, D), 1.0, 6.0, ((0, 8),))
    w_in = gaussian(key_of[1], (LAYERS, D, FFW), D ** -0.5, 0.15625, ((0, 4),))
    w_out = gaussian(key_of[2], (LAYERS, FFW, D), FFW ** -0.5, 0.109375, ((0, 4),))
    fpn_weight = gaussian(key_of[3], (2, D, CHANNELS), D ** -0.5, 0.15625, ((2, 4),))
    fc6_weight = gaussian(key_of[4], (CHANNELS, POOLED * POOLED, HEAD_UNITS), (CHANNELS * POOLED * POOLED) ** -0.5, 0.0546875, ((0, 4),))
    fc7_weight = gaussian(key_of[5], (HEAD_UNITS, HEAD_UNITS), HEAD_UNITS ** -0.5, 0.25)
    windows = draw_windows(jax.random.fold_in(key_of[10], 71), 0)
    bilinear = draw_bilinear(jax.random.fold_in(key_of[10], 71), 0)
    owners_keys = jax.random.split(jax.random.fold_in(key_of[8], 1), IMAGES * BOX_IMG // (IMG_DEV * BOX_IMG))
    owners_turns = jax.random.permutation(jax.random.fold_in(key_of[8], 3), IMAGES * BOX_IMG // (IMG_DEV * BOX_IMG))
    owners = jax.vmap(lambda own, number: routed_block(jax.random.fold_in(key_of[8], 2), own, number, IMG_DEV * BOX_IMG, OWNERS, 1, CAP, 2))(owners_keys, owners_turns).reshape((IMAGES, BOX_IMG, 1))
    cotangent = gaussian(key_of[9], (OWNERS, OWNERS, CAP, HEAD_UNITS), 1.0, 6.0, ((0, 8),))
    return {"images": images, "w_in": w_in, "w_out": w_out, "fpn_weight": fpn_weight, "fc6_weight": fc6_weight, "fc7_weight": fc7_weight, "windows": windows, "bilinear": bilinear, "owners": owners, "cotangent": cotangent}


EPS = 1e-06
GELU_C = math.sqrt(2.0 / math.pi)
HIGH = lax.Precision.HIGHEST

def gelu_parts(values):
    inner_arg = GELU_C * (values + 0.044715 * values * values * values)
    tangent = jnp.tanh(inner_arg)
    result = 0.5 * values * (1.0 + tangent)
    gelu_slope = 0.5 * (1.0 + tangent) + 0.5 * values * (1.0 - tangent * tangent) * GELU_C * (1.0 + 3.0 * 0.044715 * values * values)
    return (result, gelu_slope)

def norm_parts(tokens):
    floats = tokens.astype(jnp.float32)
    centred = floats - lax.optimization_barrier(jnp.mean(floats, axis=-1, keepdims=True))
    scale_inv = lax.rsqrt(lax.optimization_barrier(jnp.mean(centred * centred, axis=-1, keepdims=True)) + EPS)
    return (centred * scale_inv, scale_inv)

def block_forward(tokens, w_first, w_second):
    normed, scale_inv = norm_parts(tokens)
    normed_b = normed.astype(jnp.bfloat16)
    preact = jnp.dot(normed_b, w_first, preferred_element_type=jnp.float32)
    activ, gelu_slope = gelu_parts(preact)
    activ_b = activ.astype(jnp.bfloat16)
    result = (tokens.astype(jnp.float32) + jnp.dot(activ_b, w_second, preferred_element_type=jnp.float32)).astype(jnp.bfloat16)
    return (result, normed_b, preact, activ_b)

def block_backward(grad_out, tokens, preact, w_first, w_second):
    grad_act = jnp.dot(grad_out, w_second.T, preferred_element_type=jnp.float32)
    activ, gelu_slope = gelu_parts(preact)
    grad_pre = (grad_act * gelu_slope).astype(jnp.bfloat16)
    grad_norm = jnp.dot(grad_pre, w_first.T, preferred_element_type=jnp.float32)
    normed, scale_inv = norm_parts(tokens)
    grad_tok = scale_inv * (grad_norm - lax.optimization_barrier(jnp.mean(grad_norm, axis=-1, keepdims=True)) - normed * lax.optimization_barrier(jnp.mean(grad_norm * normed, axis=-1, keepdims=True)))
    return ((grad_out.astype(jnp.float32) + grad_tok).astype(jnp.bfloat16), grad_pre)

def pyramid(top_rows, fpn_first, fpn_second, images_here):
    model_width = top_rows.shape[-1]
    half_grid = GRID // 2
    grid_rows = top_rows.reshape(images_here, GRID, GRID, model_width)
    pooled = grid_rows.astype(jnp.float32).reshape(images_here, half_grid, 2, half_grid, 2, model_width).mean(axis=(2, 4)).astype(jnp.bfloat16)
    level_one = jnp.dot(pooled, fpn_second, preferred_element_type=jnp.float32)
    upsampled = jnp.repeat(jnp.repeat(level_one, 2, axis=1), 2, axis=2)
    level_zero = jnp.dot(grid_rows, fpn_first, preferred_element_type=jnp.float32) + upsampled
    return (level_zero.astype(jnp.bfloat16), level_one.astype(jnp.bfloat16), pooled)

def pyramid_back(top_rows, pooled, fpn_first, fpn_second, grad_zero, grad_one):
    images_here = pooled.shape[0]
    half_grid = pooled.shape[1]
    channels = grad_zero.shape[-1]
    model_width = top_rows.shape[-1]
    grad_one = grad_one + grad_zero.reshape(images_here, half_grid, 2, half_grid, 2, channels).sum(axis=(2, 4))
    zero_b = grad_zero.astype(jnp.bfloat16)
    one_b = grad_one.astype(jnp.bfloat16)
    grid_rows = top_rows.reshape(images_here, GRID, GRID, model_width)
    weight_zero = jnp.einsum('nyxd,nyxc->dc', grid_rows, zero_b, preferred_element_type=jnp.float32)
    weight_one = jnp.einsum('nyxd,nyxc->dc', pooled, one_b, preferred_element_type=jnp.float32)
    back_one = jnp.dot(one_b, fpn_second.T, preferred_element_type=jnp.float32)
    grad_top = jnp.dot(zero_b, fpn_first.T, preferred_element_type=jnp.float32) + 0.25 * jnp.repeat(jnp.repeat(back_one, 2, axis=1), 2, axis=2)
    return (weight_zero, weight_one, grad_top.reshape(images_here * GRID * GRID, model_width))

def window_rows(image_ids, anchor_y, anchor_x, side):
    offsets = jnp.arange(SPAN, dtype=jnp.int32)
    return image_ids[:, None, None] * (side * side) + (anchor_y[:, None, None] + offsets[None, :, None]) * side + anchor_x[:, None, None] + offsets[None, None, :]

def window_pair(image_ids, anchor_y, anchor_x):
    half_grid = GRID // 2
    near_y = jnp.minimum(anchor_y, half_grid - SPAN)
    near_x = jnp.minimum(anchor_x, half_grid - SPAN)
    return (window_rows(image_ids, anchor_y, anchor_x, GRID), window_rows(image_ids, near_y, near_x, half_grid))

def make_crops(level_zero, level_one, image_ids, levels, anchor_y, anchor_x, weights_y, weights_x):
    channels = level_zero.shape[-1]
    rows_zero, rows_one = window_pair(image_ids, anchor_y, anchor_x)
    flat_zero = level_zero.reshape(-1, channels)
    flat_one = level_one.reshape(-1, channels)
    window_cells = jnp.where((levels == 0)[:, None, None, None], flat_zero[rows_zero], flat_one[rows_one]).astype(jnp.float32)
    crop_rows = jnp.einsum('kiu,kjv,kuvc->kcij', weights_y, weights_x, window_cells, precision=HIGH)
    return crop_rows.reshape(crop_rows.shape[0], -1).astype(jnp.bfloat16)

def spread_grads(grad_crops, image_ids, levels, anchor_y, anchor_x, weights_y, weights_x, images_here, channels):
    half_grid = GRID // 2
    grad_cells = grad_crops.astype(jnp.float32).reshape(grad_crops.shape[0], channels, POOLED, POOLED)
    grad_window = jnp.einsum('kiu,kjv,kcij->kuvc', weights_y, weights_x, grad_cells, precision=HIGH)
    at_zero = (levels == 0)[:, None, None, None]
    rows_zero, rows_one = window_pair(image_ids, anchor_y, anchor_x)
    grad_zero = jnp.zeros((images_here * GRID * GRID, channels), jnp.float32).at[rows_zero.reshape(-1)].add(jnp.where(at_zero, grad_window, 0.0).reshape(-1, channels))
    grad_one = jnp.zeros((images_here * half_grid * half_grid, channels), jnp.float32).at[rows_one.reshape(-1)].add(jnp.where(at_zero, 0.0, grad_window).reshape(-1, channels))
    return (grad_zero.reshape(images_here, GRID, GRID, channels), grad_one.reshape(images_here, half_grid, half_grid, channels))

def head_pass(slot_rows, fc6_flat, fc7_weight, cot_rows):
    first_pre = jnp.dot(slot_rows, fc6_flat, preferred_element_type=jnp.float32)
    first_act, first_slope = gelu_parts(first_pre)
    first_b = first_act.astype(jnp.bfloat16)
    second_pre = jnp.dot(first_b, fc7_weight, preferred_element_type=jnp.float32)
    second_act, second_slope = gelu_parts(second_pre)
    grad_second = (cot_rows * second_slope).astype(jnp.bfloat16)
    grad_fc7 = jnp.einsum('rh,rk->hk', first_b, grad_second, preferred_element_type=jnp.float32)
    grad_first = (jnp.dot(grad_second, fc7_weight.T, preferred_element_type=jnp.float32) * first_slope).astype(jnp.bfloat16)
    grad_fc6 = jnp.einsum('rk,rh->kh', slot_rows, grad_first, preferred_element_type=jnp.float32)
    grad_slots = jnp.dot(grad_first, fc6_flat.T, preferred_element_type=jnp.float32).astype(jnp.bfloat16)
    return (grad_slots, grad_fc6, grad_fc7)

def slot_ranks(owner_ids, groups):
    onehot = (owner_ids[:, None] == jnp.arange(groups, dtype=jnp.int32)[None, :]).astype(jnp.int32)
    earlier = jnp.cumsum(onehot, axis=0) - onehot
    return lax.optimization_barrier(jnp.sum(earlier * onehot, axis=1)).astype(jnp.int32)

def rounded(values):
    return lax.optimization_barrier(values.astype(jnp.bfloat16)).astype(jnp.float32)

def reference(images, w_in, w_out, fpn_weight, fc6_weight, fc7_weight, windows, bilinear, owners, cotangent):
    groups = N_DP * N_HEAD
    layer_count = w_in.shape[0]
    fc6_flat = fc6_weight.reshape(-1, HEAD_UNITS)
    per_group = IMG_DEV * BOX_IMG

    def group_terms(group):
        first_image = group * IMG_DEV
        tokens = lax.dynamic_slice_in_dim(images, first_image, IMG_DEV, 0).reshape(IMG_DEV * GRID * GRID, D)
        saved_parts = []
        for layer_idx in range(layer_count):
            result, normed_b, preact, activ_b = block_forward(tokens, w_in[layer_idx], w_out[layer_idx])
            saved_parts.append((tokens, normed_b, preact, activ_b))
            tokens = result
        level_zero, level_one, pooled = pyramid(tokens, fpn_weight[0], fpn_weight[1], IMG_DEV)
        box_windows = lax.dynamic_slice_in_dim(windows, first_image, IMG_DEV, 1).reshape(3, per_group)
        sampling = lax.dynamic_slice_in_dim(bilinear, first_image, IMG_DEV, 3).reshape(2, POOLED, SPAN, per_group)
        weights_y = jnp.transpose(sampling[0], (2, 0, 1))
        weights_x = jnp.transpose(sampling[1], (2, 0, 1))
        image_ids = jnp.repeat(jnp.arange(IMG_DEV, dtype=jnp.int32), BOX_IMG)
        crop_rows = make_crops(level_zero, level_one, image_ids, box_windows[0], box_windows[1], box_windows[2], weights_y, weights_x)
        owner_ids = lax.dynamic_slice_in_dim(owners, first_image, IMG_DEV, 0).reshape(per_group)
        slot_rank = slot_ranks(owner_ids, groups)
        cot_rows = cotangent[owner_ids, group, slot_rank].astype(jnp.float32)
        grad_crops, grad_fc6, grad_fc7 = head_pass(crop_rows, fc6_flat, fc7_weight, cot_rows)
        grad_zero, grad_one = spread_grads(grad_crops, image_ids, box_windows[0], box_windows[1], box_windows[2], weights_y, weights_x, IMG_DEV, CHANNELS)
        weight_zero, weight_one, grad_top = pyramid_back(tokens, pooled, fpn_weight[0], fpn_weight[1], grad_zero, grad_one)
        grad_rows = grad_top.astype(jnp.bfloat16)
        firsts = [None] * layer_count
        seconds = [None] * layer_count
        for layer_idx in reversed(range(layer_count)):
            layer_in, normed_b, preact, activ_b = saved_parts[layer_idx]
            grad_in, grad_pre = block_backward(grad_rows, layer_in, preact, w_in[layer_idx], w_out[layer_idx])
            firsts[layer_idx] = rounded(jnp.dot(normed_b.T, grad_pre, preferred_element_type=jnp.float32))
            seconds[layer_idx] = rounded(jnp.dot(activ_b.T, grad_rows, preferred_element_type=jnp.float32))
            grad_rows = grad_in
        return (jnp.stack(firsts), jnp.stack(seconds), jnp.stack([weight_zero, weight_one]), grad_fc6.reshape(CHANNELS, POOLED * POOLED, HEAD_UNITS), grad_fc7)

    def accumulate(totals, group):
        new_terms = group_terms(group)
        return (jax.tree.map(lambda a, b: a + b, totals, new_terms), None)
    start_sums = (jnp.zeros((layer_count, D, FFW), jnp.float32), jnp.zeros((layer_count, FFW, D), jnp.float32), jnp.zeros((2, D, CHANNELS), jnp.float32), jnp.zeros((CHANNELS, POOLED * POOLED, HEAD_UNITS), jnp.float32), jnp.zeros((HEAD_UNITS, HEAD_UNITS), jnp.float32))
    totals, unused = lax.scan(accumulate, start_sums, jnp.arange(groups, dtype=jnp.int32))
    return (totals[0], totals[1], totals[2], totals[3], totals[4])
```

```python
import math

import jax
import jax.numpy as jnp
from jax import lax
from jax.sharding import PartitionSpec as P

GRID = 12
SPAN = 4
POOLED = 7


EPS = 1e-06
GELU_C = math.sqrt(2.0 / math.pi)
HIGH = lax.Precision.HIGHEST


def moved(block, axis, route):
    return lax.ppermute(block, axis, route)


def spread_from_last(block, axis):
    size = lax.axis_size(axis)
    place = lax.axis_index(axis)
    last = size - 1
    stride = size // 2
    while stride >= 1:
        route = [(i, i - stride) for i in range(size) if (last - i) % (2 * stride) == 0]
        arrived = moved(block, axis, route)
        takes = (last - place) % (2 * stride) == stride
        block = jnp.where(takes, arrived, block)
        stride //= 2
    return block


def sum_to_last(block, axis):
    size = lax.axis_size(axis)
    last = size - 1
    total = block.astype(jnp.float32)
    stride = 1
    while stride < size:
        route = [(i - stride, i) for i in range(size) if (last - i) % (2 * stride) == 0]
        arrived = moved(total.astype(jnp.bfloat16), axis, route)
        total = total + arrived.astype(jnp.float32)
        stride *= 2
    return total.astype(jnp.bfloat16)


def sum_everywhere(block, axis):
    size = lax.axis_size(axis)
    terms = [block] + [
        moved(block, axis, [(i, i ^ distance) for i in range(size)]) for distance in range(1, size)
    ]
    terms = [term.astype(jnp.float32) for term in terms]
    while len(terms) > 1:
        terms = [terms[i] + terms[i + 1] for i in range(0, len(terms), 2)]
    return terms[0]


def gelu_parts(values):
    inner_arg = GELU_C * (values + 0.044715 * values * values * values)
    tangent = jnp.tanh(inner_arg)
    result = 0.5 * values * (1.0 + tangent)
    gelu_slope = 0.5 * (1.0 + tangent) + 0.5 * values * (1.0 - tangent * tangent) * GELU_C * (
        1.0 + 3.0 * 0.044715 * values * values
    )
    return (result, gelu_slope)


def norm_parts(tokens):
    floats = tokens.astype(jnp.float32)
    centred = floats - jnp.mean(floats, axis=-1, keepdims=True)
    scale_inv = lax.rsqrt(jnp.mean(centred * centred, axis=-1, keepdims=True) + EPS)
    return (centred * scale_inv, scale_inv)


def dot(left, right):
    return jnp.dot(left, right, preferred_element_type=jnp.float32)


def dot_nt(left, right):
    return jnp.einsum("rk,ck->rc", left, right, preferred_element_type=jnp.float32)


def dot_tn(left, right):
    return jnp.einsum("kr,kc->rc", left, right, preferred_element_type=jnp.float32)


def block_forward(tokens, w_first, w_second):
    normed, scale_inv = norm_parts(tokens)
    activ, gelu_slope = gelu_parts(dot(normed.astype(jnp.bfloat16), w_first))
    return (tokens.astype(jnp.float32) + dot(activ.astype(jnp.bfloat16), w_second)).astype(
        jnp.bfloat16
    )


def block_backward(grad_out, normed, scale_inv, slope, w_first, w_second):
    grad_pre = (dot_nt(grad_out, w_second) * slope).astype(jnp.bfloat16)
    grad_norm = dot_nt(grad_pre, w_first)
    grad_tok = scale_inv * (
        grad_norm
        - jnp.mean(grad_norm, axis=-1, keepdims=True)
        - normed * jnp.mean(grad_norm * normed, axis=-1, keepdims=True)
    )
    return (grad_out.astype(jnp.float32) + grad_tok).astype(jnp.bfloat16)


def parents():
    half = GRID // 2
    cells = jnp.arange(GRID * GRID, dtype=jnp.int32)
    parent = (cells // GRID // 2) * half + (cells % GRID) // 2
    return (parent[:, None] == jnp.arange(half * half, dtype=jnp.int32)[None, :])


def sampling_rows(windows, bilinear):
    half = GRID // 2
    levels, anchor_y, anchor_x = (windows[i][:, None] for i in range(3))
    fine = jnp.arange(GRID * GRID, dtype=jnp.int32)
    coarse = jnp.arange(half * half, dtype=jnp.int32)
    cell_level = jnp.concatenate([jnp.zeros_like(fine), jnp.ones_like(coarse)])[None]
    cell_y = jnp.concatenate([fine // GRID, coarse // half])[None]
    cell_x = jnp.concatenate([fine % GRID, coarse % half])[None]
    offset_y = jnp.where(levels == cell_level, cell_y - anchor_y, -1)
    offset_x = cell_x - anchor_x
    rows = sum(
        bilinear[0][:, u, :, None] * (offset_y == u).astype(jnp.float32)[None] for u in range(SPAN)
    )
    cols = sum(
        bilinear[1][:, v, :, None] * (offset_x == v).astype(jnp.float32)[None] for v in range(SPAN)
    )
    weights = (rows[:, None] * cols[None]).astype(jnp.bfloat16)
    return weights.reshape(-1, weights.shape[-1])


def box_cotangents(cotangent, owner_ids):
    groups, capacity, units = cotangent.shape
    arrived = lax.all_to_all(cotangent, ("dp", "head"), split_axis=0, concat_axis=0, tiled=True)
    count = owner_ids.shape[0]
    order = jnp.arange(count, dtype=jnp.int32)
    earlier = (owner_ids[:, None] == owner_ids[None, :]) & (order[None, :] < order[:, None])
    rank = jnp.sum(earlier.astype(jnp.int32), axis=1)
    slot = owner_ids * capacity + rank
    pick = slot[:, None] == jnp.arange(groups * capacity, dtype=jnp.int32)[None, :]
    return dot(pick.astype(jnp.bfloat16), arrived.reshape(groups * capacity, units))


def per_device(
    images, w_in, w_out, fpn_weight, fc6_weight, fc7_weight, windows, bilinear, owners, cotangent
):
    axes = ("dp", "head")
    sections = lax.axis_size("section")
    section_idx = lax.axis_index("section")
    groups = lax.axis_size(axes)
    group_idx = lax.axis_index(axes)
    last_section = sections - 1
    w_first = w_in[0]
    w_second = w_out[0]
    model_width, inner_width = w_first.shape
    channels = fpn_weight.shape[2]
    head_units = fc7_weight.shape[0]
    boxes = windows.shape[2]
    taps = POOLED * POOLED
    fine_cells = GRID * GRID

    cot_rows = box_cotangents(cotangent[0], owners.reshape(boxes))
    weights = sampling_rows(windows[:, 0], bilinear[:, :, :, 0])
    fc6_taps = jnp.transpose(fc6_weight, (1, 0, 2)).reshape(taps * channels, head_units)

    tokens = images[0]
    kept_tokens = tokens
    for step in range(sections):
        if step:
            route = [(i, i + 1) for i in range(sections - 1)]
            tokens = moved(result, "section", route)
            kept_tokens = jnp.where(section_idx == step, tokens, kept_tokens)
        result = block_forward(tokens, w_first, w_second)
    top = spread_from_last(result, "section")

    all_tokens = lax.all_gather(kept_tokens, axes, axis=0, tiled=True)

    up = parents()
    up_b = up.astype(jnp.bfloat16)
    up_f = up.astype(jnp.float32)
    pooled = (0.25 * dot_tn(up_b, top)).astype(jnp.bfloat16)
    level_one = dot(pooled, fpn_weight[1])
    level_zero = dot(top, fpn_weight[0]) + jnp.dot(up_f, level_one, precision=HIGH)
    cells = jnp.concatenate([level_zero, level_one], axis=0).astype(jnp.bfloat16)
    crops = dot(weights, cells).astype(jnp.bfloat16).reshape(taps, boxes, channels)
    crop_rows = jnp.transpose(crops, (1, 0, 2)).reshape(boxes, taps * channels)
    first_pre = sum_everywhere(dot(crop_rows, fc6_taps).astype(jnp.bfloat16), "section")

    normed_own, scale_own = norm_parts(kept_tokens)
    slope_own = gelu_parts(dot(normed_own.astype(jnp.bfloat16), w_first))[1]

    first_act, first_slope = gelu_parts(first_pre)
    first_b = first_act.astype(jnp.bfloat16)
    second_slope = gelu_parts(dot(first_b, fc7_weight))[1]
    grad_second = (cot_rows * second_slope).astype(jnp.bfloat16)
    grad_first = (dot_nt(grad_second, fc7_weight) * first_slope).astype(jnp.bfloat16)
    grad_crops = dot_nt(grad_first, fc6_taps).astype(jnp.bfloat16)
    grad_crops = jnp.transpose(grad_crops.reshape(boxes, taps, channels), (1, 0, 2))
    grad_cells = dot_tn(weights, grad_crops.reshape(taps * boxes, channels))
    grad_zero = grad_cells[:fine_cells]
    zero_b = grad_zero.astype(jnp.bfloat16)
    one_b = (
        grad_cells[fine_cells:] + jnp.einsum("kr,kc->rc", up_f, grad_zero, precision=HIGH)
    ).astype(jnp.bfloat16)
    both = jnp.concatenate([zero_b, (0.25 * dot(up_b, one_b)).astype(jnp.bfloat16)], axis=1)
    both_weights = jnp.concatenate([fpn_weight[0], fpn_weight[1]], axis=1)
    grad_out = sum_to_last(dot_nt(both, both_weights), "section")

    grad_fc6 = dot_tn(grad_first, crop_rows).astype(jnp.bfloat16)
    fc6_part = lax.psum_scatter(grad_fc6, axes, scatter_dimension=0, tiled=True)
    grad_fc7 = dot_tn(grad_second, first_b).astype(jnp.bfloat16)
    fc7_part = lax.psum_scatter(grad_fc7, axes, scatter_dimension=0, tiled=True)
    fpn_terms = jnp.stack([dot_tn(top, zero_b), dot_tn(pooled, one_b)])
    grad_fpn = lax.psum(fpn_terms.astype(jnp.bfloat16), axes).astype(jnp.float32)

    kept_grad = grad_out
    for step in range(sections - 1):
        grad_in = block_backward(grad_out, normed_own, scale_own, slope_own, w_first, w_second)
        grad_out = moved(grad_in, "section", [(i + 1, i) for i in range(sections - 1)])
        kept_grad = jnp.where(section_idx == last_section - 1 - step, grad_out, kept_grad)
    all_grads = lax.all_gather(kept_grad, axes, axis=0, tiled=True)

    all_normed = norm_parts(all_tokens)[0].astype(jnp.bfloat16)
    all_slopes = gelu_parts(dot(all_normed, w_first))[1].astype(jnp.bfloat16)
    inner_part = inner_width // groups
    width_part = model_width // groups
    w_part = lax.dynamic_slice_in_dim(w_first, group_idx * inner_part, inner_part, 1)
    act_part = gelu_parts(dot(all_normed, w_part))[0].astype(jnp.bfloat16)
    normed_part = lax.dynamic_slice_in_dim(all_normed, group_idx * width_part, width_part, 1)
    all_slopes, act_part, normed_part, all_grads = lax.optimization_barrier(
        (all_slopes, act_part, normed_part, all_grads)
    )
    grad_pre = (dot_nt(all_grads, w_second) * all_slopes.astype(jnp.float32)).astype(jnp.bfloat16)
    grad_first_w = dot_tn(normed_part, grad_pre)
    grad_second_w = dot_tn(act_part, all_grads)

    fc6_out = jnp.transpose(
        fc6_part.astype(jnp.float32).reshape(-1, taps, channels), (2, 1, 0)
    )
    fc7_out = jnp.transpose(fc7_part.astype(jnp.float32))
    return (grad_first_w[None], grad_second_w[None], grad_fpn, fc6_out, fc7_out)


def solution(mesh):
    return jax.shard_map(
        per_device,
        mesh=mesh,
        in_specs=(
            P(("dp", "head"), None, None),
            P("section", None, None),
            P("section", None, None),
            P(None, None, "section"),
            P("section", None, None),
            P(),
            P(None, ("dp", "head"), None),
            P(None, None, None, ("dp", "head"), None),
            P(("dp", "head"), None, None),
            P(("dp", "head"), None, None, None),
        ),
        out_specs=(
            P("section", ("dp", "head"), None),
            P("section", ("dp", "head"), None),
            P(None, None, "section"),
            P("section", None, ("dp", "head")),
            P(None, ("dp", "head")),
        ),
        check_vma=False,
    )
```

```python
import math

import jax
import jax.numpy as jnp
from jax import lax
from jax.sharding import PartitionSpec as P

GRID = 12
SPAN = 4
POOLED = 7


EPS = 1e-06
GELU_C = math.sqrt(2.0 / math.pi)
HIGH = lax.Precision.HIGHEST


def moved(block, axis, route):
    return lax.ppermute(block, axis, route)


def spread_from_last(block, axis):
    size = lax.axis_size(axis)
    place = lax.axis_index(axis)
    last = size - 1
    stride = size // 2
    while stride >= 1:
        route = [(i, i - stride) for i in range(size) if (last - i) % (2 * stride) == 0]
        arrived = moved(block, axis, route)
        takes = (last - place) % (2 * stride) == stride
        block = jnp.where(takes, arrived, block)
        stride //= 2
    return block


def sum_to_last(block, axis):
    size = lax.axis_size(axis)
    last = size - 1
    total = block.astype(jnp.float32)
    stride = 1
    while stride < size:
        route = [(i - stride, i) for i in range(size) if (last - i) % (2 * stride) == 0]
        arrived = moved(total.astype(jnp.bfloat16), axis, route)
        total = total + arrived.astype(jnp.float32)
        stride *= 2
    return total.astype(jnp.bfloat16)


def sum_everywhere(block, axis):
    size = lax.axis_size(axis)
    terms = [block] + [
        moved(block, axis, [(i, i ^ distance) for i in range(size)]) for distance in range(1, size)
    ]
    terms = [term.astype(jnp.float32) for term in terms]
    while len(terms) > 1:
        terms = [terms[i] + terms[i + 1] for i in range(0, len(terms), 2)]
    return terms[0]


def gelu_parts(values):
    inner_arg = GELU_C * (values + 0.044715 * values * values * values)
    tangent = jnp.tanh(inner_arg)
    result = 0.5 * values * (1.0 + tangent)
    gelu_slope = 0.5 * (1.0 + tangent) + 0.5 * values * (1.0 - tangent * tangent) * GELU_C * (
        1.0 + 3.0 * 0.044715 * values * values
    )
    return (result, gelu_slope)


def norm_parts(tokens):
    floats = tokens.astype(jnp.float32)
    centred = floats - jnp.mean(floats, axis=-1, keepdims=True)
    scale_inv = lax.rsqrt(jnp.mean(centred * centred, axis=-1, keepdims=True) + EPS)
    return (centred * scale_inv, scale_inv)


def dot(left, right):
    return jnp.dot(left, right, preferred_element_type=jnp.float32)


def dot_nt(left, right):
    return jnp.einsum("rk,ck->rc", left, right, preferred_element_type=jnp.float32)


def dot_tn(left, right):
    return jnp.einsum("kr,kc->rc", left, right, preferred_element_type=jnp.float32)


def block_forward(tokens, w_first, w_second):
    normed, scale_inv = norm_parts(tokens)
    activ, gelu_slope = gelu_parts(dot(normed.astype(jnp.bfloat16), w_first))
    activ_b = lax.optimization_barrier(activ.astype(jnp.bfloat16))
    return (tokens.astype(jnp.float32) + dot(activ_b, w_second)).astype(jnp.bfloat16)


def block_backward(grad_out, normed, scale_inv, slope, w_first, w_second):
    grad_pre = (dot_nt(grad_out, w_second) * slope).astype(jnp.bfloat16)
    grad_pre = lax.optimization_barrier(grad_pre)
    grad_norm = dot_nt(grad_pre, w_first)
    grad_tok = scale_inv * (
        grad_norm
        - jnp.mean(grad_norm, axis=-1, keepdims=True)
        - normed * jnp.mean(grad_norm * normed, axis=-1, keepdims=True)
    )
    return (grad_out.astype(jnp.float32) + grad_tok).astype(jnp.bfloat16)


def parents():
    half = GRID // 2
    cells = jnp.arange(GRID * GRID, dtype=jnp.int32)
    parent = (cells // GRID // 2) * half + (cells % GRID) // 2
    return (parent[:, None] == jnp.arange(half * half, dtype=jnp.int32)[None, :])


def sampling_rows(windows, bilinear):
    half = GRID // 2
    levels, anchor_y, anchor_x = (windows[i][:, None] for i in range(3))
    fine = jnp.arange(GRID * GRID, dtype=jnp.int32)
    coarse = jnp.arange(half * half, dtype=jnp.int32)
    cell_level = jnp.concatenate([jnp.zeros_like(fine), jnp.ones_like(coarse)])[None]
    cell_y = jnp.concatenate([fine // GRID, coarse // half])[None]
    cell_x = jnp.concatenate([fine % GRID, coarse % half])[None]
    offset_y = jnp.where(levels == cell_level, cell_y - anchor_y, -1)
    offset_x = cell_x - anchor_x
    rows = sum(
        bilinear[0][:, u, :, None] * (offset_y == u).astype(jnp.float32)[None] for u in range(SPAN)
    )
    cols = sum(
        bilinear[1][:, v, :, None] * (offset_x == v).astype(jnp.float32)[None] for v in range(SPAN)
    )
    weights = (rows[:, None] * cols[None]).astype(jnp.bfloat16)
    return weights.reshape(-1, weights.shape[-1])


def box_cotangents(cotangent, owner_ids):
    groups, capacity, units = cotangent.shape
    arrived = lax.all_to_all(cotangent, ("dp", "head"), split_axis=0, concat_axis=0, tiled=True)
    count = owner_ids.shape[0]
    order = jnp.arange(count, dtype=jnp.int32)
    earlier = (owner_ids[:, None] == owner_ids[None, :]) & (order[None, :] < order[:, None])
    rank = jnp.sum(earlier.astype(jnp.int32), axis=1)
    slot = owner_ids * capacity + rank
    pick = slot[:, None] == jnp.arange(groups * capacity, dtype=jnp.int32)[None, :]
    return dot(pick.astype(jnp.bfloat16), arrived.reshape(groups * capacity, units))


def per_device(
    images, w_in, w_out, fpn_weight, fc6_weight, fc7_weight, windows, bilinear, owners, cotangent
):
    axes = ("dp", "head")
    sections = lax.axis_size("section")
    section_idx = lax.axis_index("section")
    groups = lax.axis_size(axes)
    group_idx = lax.axis_index(axes)
    last_section = sections - 1
    w_first = w_in[0]
    w_second = w_out[0]
    model_width, inner_width = w_first.shape
    channels = fpn_weight.shape[2]
    head_units = fc7_weight.shape[0]
    boxes = windows.shape[2]
    taps = POOLED * POOLED
    fine_cells = GRID * GRID

    cot_rows = box_cotangents(cotangent[0], owners.reshape(boxes))
    weights = sampling_rows(windows[:, 0], bilinear[:, :, :, 0])
    fc6_taps = jnp.transpose(fc6_weight, (1, 0, 2)).reshape(taps * channels, head_units)

    tokens = images[0]
    kept_tokens = tokens
    for step in range(sections):
        if step:
            route = [(i, i + 1) for i in range(sections - 1)]
            tokens = moved(result, "section", route)
            kept_tokens = jnp.where(section_idx == step, tokens, kept_tokens)
        result = block_forward(tokens, w_first, w_second)
    top = spread_from_last(result, "section")

    all_tokens = lax.all_gather(kept_tokens, axes, axis=0, tiled=True)

    up = parents()
    up_b = up.astype(jnp.bfloat16)
    up_f = up.astype(jnp.float32)
    pooled = (0.25 * dot_tn(up_b, top)).astype(jnp.bfloat16)
    level_one = dot(pooled, fpn_weight[1])
    level_zero = dot(top, fpn_weight[0]) + jnp.dot(up_f, level_one, precision=HIGH)
    cells = jnp.concatenate([level_zero, level_one], axis=0).astype(jnp.bfloat16)
    crops = dot(weights, cells).astype(jnp.bfloat16).reshape(taps, boxes, channels)
    crop_rows = jnp.transpose(crops, (1, 0, 2)).reshape(boxes, taps * channels)
    first_pre = sum_everywhere(dot(crop_rows, fc6_taps).astype(jnp.bfloat16), "section")

    normed_own, scale_own = norm_parts(kept_tokens)
    slope_own = gelu_parts(dot(normed_own.astype(jnp.bfloat16), w_first))[1]

    first_act, first_slope = gelu_parts(first_pre)
    first_b = first_act.astype(jnp.bfloat16)
    second_slope = gelu_parts(dot(first_b, fc7_weight))[1]
    grad_second = (cot_rows * second_slope).astype(jnp.bfloat16)
    grad_first = (dot_nt(grad_second, fc7_weight) * first_slope).astype(jnp.bfloat16)
    grad_crops = dot_nt(grad_first, fc6_taps).astype(jnp.bfloat16)
    grad_crops = jnp.transpose(grad_crops.reshape(boxes, taps, channels), (1, 0, 2))
    grad_cells = dot_tn(weights, grad_crops.reshape(taps * boxes, channels))
    grad_zero = grad_cells[:fine_cells]
    zero_b = grad_zero.astype(jnp.bfloat16)
    one_b = (
        grad_cells[fine_cells:] + jnp.einsum("kr,kc->rc", up_f, grad_zero, precision=HIGH)
    ).astype(jnp.bfloat16)
    both = jnp.concatenate([zero_b, (0.25 * dot(up_b, one_b)).astype(jnp.bfloat16)], axis=1)
    both_weights = jnp.concatenate([fpn_weight[0], fpn_weight[1]], axis=1)
    top_part = dot_nt(both, both_weights)

    fpn_terms = jnp.concatenate([dot_tn(zero_b, top), dot_tn(one_b, pooled)], axis=0)
    terms = jnp.concatenate(
        [
            dot_tn(grad_first, crop_rows).astype(jnp.bfloat16),
            dot_tn(grad_second, first_b).astype(jnp.bfloat16),
            fpn_terms.astype(jnp.bfloat16).reshape(head_units, -1),
        ],
        axis=1,
    )
    terms, all_tokens, top_part = lax.optimization_barrier((terms, all_tokens, top_part))
    part = lax.psum_scatter(terms, axes, scatter_dimension=0, tiled=True)
    fc6_part = part[:, : taps * channels]
    fc7_part = part[:, taps * channels : taps * channels + head_units]
    fpn_part = part[:, taps * channels + head_units :].reshape(-1, model_width)

    grad_out = sum_to_last(top_part, "section")
    kept_grad = grad_out
    for step in range(sections - 1):
        grad_in = block_backward(grad_out, normed_own, scale_own, slope_own, w_first, w_second)
        grad_out = moved(grad_in, "section", [(i + 1, i) for i in range(sections - 1)])
        kept_grad = jnp.where(section_idx == last_section - 1 - step, grad_out, kept_grad)
    token_rows = kept_grad.shape[0]
    arrived = lax.all_gather(jnp.concatenate([kept_grad, fpn_part], axis=0), axes, axis=0)
    all_grads = arrived[:, :token_rows].reshape(-1, model_width)
    grad_fpn = arrived[:, token_rows:].reshape(2, channels, model_width).astype(jnp.float32)
    grad_fpn = jnp.transpose(grad_fpn, (0, 2, 1))

    all_normed = norm_parts(all_tokens)[0].astype(jnp.bfloat16)
    all_slopes = gelu_parts(dot(all_normed, w_first))[1].astype(jnp.bfloat16)
    inner_part = inner_width // groups
    width_part = model_width // groups
    w_part = lax.dynamic_slice_in_dim(w_first, group_idx * inner_part, inner_part, 1)
    act_part = gelu_parts(dot(all_normed, w_part))[0].astype(jnp.bfloat16)
    normed_part = lax.dynamic_slice_in_dim(all_normed, group_idx * width_part, width_part, 1)
    all_slopes, act_part, normed_part, all_grads = lax.optimization_barrier(
        (all_slopes, act_part, normed_part, all_grads)
    )
    grad_pre = (dot_nt(all_grads, w_second) * all_slopes.astype(jnp.float32)).astype(jnp.bfloat16)
    grad_first_w = dot_tn(normed_part, grad_pre)
    grad_second_w = dot_tn(act_part, all_grads)

    fc6_out = jnp.transpose(
        fc6_part.astype(jnp.float32).reshape(-1, taps, channels), (2, 1, 0)
    )
    fc7_out = jnp.transpose(fc7_part.astype(jnp.float32))
    return (grad_first_w[None], grad_second_w[None], grad_fpn, fc6_out, fc7_out)


def solution(mesh):
    return jax.shard_map(
        per_device,
        mesh=mesh,
        in_specs=(
            P(("dp", "head"), None, None),
            P("section", None, None),
            P("section", None, None),
            P(None, None, "section"),
            P("section", None, None),
            P(),
            P(None, ("dp", "head"), None),
            P(None, None, None, ("dp", "head"), None),
            P(("dp", "head"), None, None),
            P(("dp", "head"), None, None, None),
        ),
        out_specs=(
            P("section", ("dp", "head"), None),
            P("section", ("dp", "head"), None),
            P(None, None, "section"),
            P("section", None, ("dp", "head")),
            P(None, ("dp", "head")),
        ),
        check_vma=False,
    )
```

```python
import math

import jax
import jax.numpy as jnp
from jax import lax
from jax.sharding import PartitionSpec as P

GRID = 12
SPAN = 4
POOLED = 7


EPS = 1e-06
GELU_C = math.sqrt(2.0 / math.pi)
HIGH = lax.Precision.HIGHEST


def moved(block, axis, route):
    return lax.ppermute(block, axis, route)


def spread_from_last(block, axis):
    size = lax.axis_size(axis)
    place = lax.axis_index(axis)
    last = size - 1
    stride = size // 2
    while stride >= 1:
        route = [(i, i - stride) for i in range(size) if (last - i) % (2 * stride) == 0]
        arrived = moved(block, axis, route)
        takes = (last - place) % (2 * stride) == stride
        block = jnp.where(takes, arrived, block)
        stride //= 2
    return block


def sum_to_last(block, axis):
    size = lax.axis_size(axis)
    last = size - 1
    total = block.astype(jnp.float32)
    stride = 1
    while stride < size:
        route = [(i - stride, i) for i in range(size) if (last - i) % (2 * stride) == 0]
        arrived = moved(total.astype(jnp.bfloat16), axis, route)
        total = total + arrived.astype(jnp.float32)
        stride *= 2
    return total.astype(jnp.bfloat16)


def sum_everywhere(block, axis):
    size = lax.axis_size(axis)
    terms = [block] + [
        moved(block, axis, [(i, i ^ distance) for i in range(size)]) for distance in range(1, size)
    ]
    terms = [term.astype(jnp.float32) for term in terms]
    while len(terms) > 1:
        terms = [terms[i] + terms[i + 1] for i in range(0, len(terms), 2)]
    return terms[0]


def summed_share(blocks, axes):
    arrived = lax.all_to_all(blocks, axes, split_axis=0, concat_axis=0, tiled=True)
    return jnp.sum(arrived.astype(jnp.float32), axis=0)


def gelu_parts(values):
    inner_arg = GELU_C * (values + 0.044715 * values * values * values)
    tangent = jnp.tanh(inner_arg)
    result = 0.5 * values * (1.0 + tangent)
    gelu_slope = 0.5 * (1.0 + tangent) + 0.5 * values * (1.0 - tangent * tangent) * GELU_C * (
        1.0 + 3.0 * 0.044715 * values * values
    )
    return (result, gelu_slope)


def norm_parts(tokens):
    floats = tokens.astype(jnp.float32)
    centred = floats - jnp.mean(floats, axis=-1, keepdims=True)
    scale_inv = lax.rsqrt(jnp.mean(centred * centred, axis=-1, keepdims=True) + EPS)
    return (centred * scale_inv, scale_inv)


def dot(left, right):
    return jnp.dot(left, right, preferred_element_type=jnp.float32)


def dot_nt(left, right):
    return jnp.einsum("rk,ck->rc", left, right, preferred_element_type=jnp.float32)


def dot_tn(left, right):
    return jnp.einsum("kr,kc->rc", left, right, preferred_element_type=jnp.float32)


def block_forward(tokens, w_first, w_second):
    normed, scale_inv = norm_parts(tokens)
    activ, gelu_slope = gelu_parts(dot(normed.astype(jnp.bfloat16), w_first))
    activ_b = lax.optimization_barrier(activ.astype(jnp.bfloat16))
    return (tokens.astype(jnp.float32) + dot(activ_b, w_second)).astype(jnp.bfloat16)


def block_backward(grad_out, normed, scale_inv, slope, w_first, w_second):
    grad_pre = (dot_nt(grad_out, w_second) * slope).astype(jnp.bfloat16)
    grad_pre = lax.optimization_barrier(grad_pre)
    grad_norm = dot_nt(grad_pre, w_first)
    grad_tok = scale_inv * (
        grad_norm
        - jnp.mean(grad_norm, axis=-1, keepdims=True)
        - normed * jnp.mean(grad_norm * normed, axis=-1, keepdims=True)
    )
    return (grad_out.astype(jnp.float32) + grad_tok).astype(jnp.bfloat16)


def parents():
    half = GRID // 2
    cells = jnp.arange(GRID * GRID, dtype=jnp.int32)
    parent = (cells // GRID // 2) * half + (cells % GRID) // 2
    return (parent[:, None] == jnp.arange(half * half, dtype=jnp.int32)[None, :])


def sampling_rows(windows, bilinear):
    half = GRID // 2
    levels, anchor_y, anchor_x = (windows[i][:, None] for i in range(3))
    fine = jnp.arange(GRID * GRID, dtype=jnp.int32)
    coarse = jnp.arange(half * half, dtype=jnp.int32)
    cell_level = jnp.concatenate([jnp.zeros_like(fine), jnp.ones_like(coarse)])[None]
    cell_y = jnp.concatenate([fine // GRID, coarse // half])[None]
    cell_x = jnp.concatenate([fine % GRID, coarse % half])[None]
    offset_y = jnp.where(levels == cell_level, cell_y - anchor_y, -1)
    offset_x = cell_x - anchor_x
    rows = sum(
        bilinear[0][:, u, :, None] * (offset_y == u).astype(jnp.float32)[None] for u in range(SPAN)
    )
    cols = sum(
        bilinear[1][:, v, :, None] * (offset_x == v).astype(jnp.float32)[None] for v in range(SPAN)
    )
    weights = (rows[:, None] * cols[None]).astype(jnp.bfloat16)
    return weights.reshape(-1, weights.shape[-1])


def box_cotangents(cotangent, owner_ids):
    groups, capacity, units = cotangent.shape
    arrived = lax.all_to_all(cotangent, ("dp", "head"), split_axis=0, concat_axis=0, tiled=True)
    count = owner_ids.shape[0]
    order = jnp.arange(count, dtype=jnp.int32)
    earlier = (owner_ids[:, None] == owner_ids[None, :]) & (order[None, :] < order[:, None])
    rank = jnp.sum(earlier.astype(jnp.int32), axis=1)
    slot = owner_ids * capacity + rank
    pick = slot[:, None] == jnp.arange(groups * capacity, dtype=jnp.int32)[None, :]
    return dot(pick.astype(jnp.bfloat16), arrived.reshape(groups * capacity, units))


def per_device(
    images, w_in, w_out, fpn_weight, fc6_weight, fc7_weight, windows, bilinear, owners, cotangent
):
    axes = ("dp", "head")
    sections = lax.axis_size("section")
    section_idx = lax.axis_index("section")
    groups = lax.axis_size(axes)
    group_idx = lax.axis_index(axes)
    last_section = sections - 1
    w_first = w_in[0]
    w_second = w_out[0]
    model_width, inner_width = w_first.shape
    channels = fpn_weight.shape[2]
    head_units = fc7_weight.shape[0]
    boxes = windows.shape[2]
    taps = POOLED * POOLED
    fine_cells = GRID * GRID

    cot_rows = box_cotangents(cotangent[0], owners.reshape(boxes))
    weights = sampling_rows(windows[:, 0], bilinear[:, :, :, 0])
    fc6_taps = jnp.transpose(fc6_weight, (1, 0, 2)).reshape(taps * channels, head_units)

    tokens = images[0]
    kept_tokens = tokens
    for step in range(sections):
        if step:
            route = [(i, i + 1) for i in range(sections - 1)]
            tokens = moved(result, "section", route)
            kept_tokens = jnp.where(section_idx == step, tokens, kept_tokens)
        result = block_forward(tokens, w_first, w_second)
    top = spread_from_last(result, "section")

    all_tokens = lax.all_gather(kept_tokens, axes, axis=0, tiled=True)

    up = parents()
    up_b = up.astype(jnp.bfloat16)
    up_f = up.astype(jnp.float32)
    pooled = (0.25 * dot_tn(up_b, top)).astype(jnp.bfloat16)
    level_one = dot(pooled, fpn_weight[1])
    level_zero = dot(top, fpn_weight[0]) + jnp.dot(up_f, level_one, precision=HIGH)
    cells = jnp.concatenate([level_zero, level_one], axis=0).astype(jnp.bfloat16)
    crops = dot(weights, cells).astype(jnp.bfloat16).reshape(taps, boxes, channels)
    crop_rows = jnp.transpose(crops, (1, 0, 2)).reshape(boxes, taps * channels)
    first_pre = sum_everywhere(dot(crop_rows, fc6_taps).astype(jnp.bfloat16), "section")

    normed_own, scale_own = norm_parts(kept_tokens)
    slope_own = gelu_parts(dot(normed_own.astype(jnp.bfloat16), w_first))[1]

    first_act, first_slope = gelu_parts(first_pre)
    first_b = first_act.astype(jnp.bfloat16)
    second_slope = gelu_parts(dot(first_b, fc7_weight))[1]
    grad_second = (cot_rows * second_slope).astype(jnp.bfloat16)
    grad_first = (dot_nt(grad_second, fc7_weight) * first_slope).astype(jnp.bfloat16)
    grad_crops = dot_nt(grad_first, fc6_taps).astype(jnp.bfloat16)
    grad_crops = jnp.transpose(grad_crops.reshape(boxes, taps, channels), (1, 0, 2))
    grad_cells = dot_tn(weights, grad_crops.reshape(taps * boxes, channels))
    grad_zero = grad_cells[:fine_cells]
    zero_b = grad_zero.astype(jnp.bfloat16)
    one_b = (
        grad_cells[fine_cells:] + jnp.einsum("kr,kc->rc", up_f, grad_zero, precision=HIGH)
    ).astype(jnp.bfloat16)
    both = jnp.concatenate([zero_b, (0.25 * dot(up_b, one_b)).astype(jnp.bfloat16)], axis=1)
    both_weights = jnp.concatenate([fpn_weight[0], fpn_weight[1]], axis=1)
    top_part = dot_nt(both, both_weights)

    fpn_terms = jnp.concatenate([dot_tn(zero_b, top), dot_tn(one_b, pooled)], axis=0)
    fpn_rows = 2 * channels // groups
    grad_fc7 = dot_tn(grad_second, first_b).astype(jnp.bfloat16)
    fc7_tall = grad_fc7.reshape(groups, -1, fpn_rows, head_units)
    small = jnp.concatenate(
        [fpn_terms.astype(jnp.bfloat16).reshape(groups, fpn_rows, model_width)]
        + [fc7_tall[:, q] for q in range(fc7_tall.shape[1])],
        axis=-1,
    )
    grad_fc6 = dot_tn(grad_first, crop_rows).astype(jnp.bfloat16)
    grad_fc6 = grad_fc6.reshape(groups, -1, taps * channels)
    small, grad_fc6, top_part = lax.optimization_barrier((small, grad_fc6, top_part))
    small_part = summed_share(small, axes)
    fc6_blocks = lax.all_to_all(grad_fc6, axes, split_axis=0, concat_axis=0, tiled=True)
    fpn_part = small_part[:, :model_width].astype(jnp.bfloat16)
    fc7_part = jnp.concatenate(
        [
            small_part[:, model_width + q * head_units : model_width + (q + 1) * head_units]
            for q in range(fc7_tall.shape[1])
        ],
        axis=0,
    )

    grad_out = sum_to_last(top_part, "section")
    kept_grad = grad_out
    for step in range(sections - 1):
        grad_in = block_backward(grad_out, normed_own, scale_own, slope_own, w_first, w_second)
        grad_out = moved(grad_in, "section", [(i + 1, i) for i in range(sections - 1)])
        kept_grad = jnp.where(section_idx == last_section - 1 - step, grad_out, kept_grad)
    kept_grad, fc6_blocks = lax.optimization_barrier((kept_grad, fc6_blocks))
    fc6_part = jnp.sum(fc6_blocks.astype(jnp.float32), axis=0)
    token_rows = kept_grad.shape[0]
    arrived = lax.all_gather(jnp.concatenate([kept_grad, fpn_part], axis=0), axes, axis=0)
    all_grads = arrived[:, :token_rows].reshape(-1, model_width)
    grad_fpn = arrived[:, token_rows:].reshape(2, channels, model_width).astype(jnp.float32)
    grad_fpn = jnp.transpose(grad_fpn, (0, 2, 1))

    all_normed = norm_parts(all_tokens)[0].astype(jnp.bfloat16)
    all_slopes = gelu_parts(dot(all_normed, w_first))[1].astype(jnp.bfloat16)
    inner_part = inner_width // groups
    width_part = model_width // groups
    w_part = lax.dynamic_slice_in_dim(w_first, group_idx * inner_part, inner_part, 1)
    act_part = gelu_parts(dot(all_normed, w_part))[0].astype(jnp.bfloat16)
    normed_part = lax.dynamic_slice_in_dim(all_normed, group_idx * width_part, width_part, 1)
    all_slopes, act_part, normed_part, all_grads = lax.optimization_barrier(
        (all_slopes, act_part, normed_part, all_grads)
    )
    grad_pre = (dot_nt(all_grads, w_second) * all_slopes.astype(jnp.float32)).astype(jnp.bfloat16)
    grad_first_w = dot_tn(normed_part, grad_pre)
    grad_second_w = dot_tn(act_part, all_grads)

    fc6_out = jnp.transpose(
        fc6_part.reshape(-1, taps, channels), (2, 1, 0)
    )
    fc7_out = jnp.transpose(fc7_part)
    return (grad_first_w[None], grad_second_w[None], grad_fpn, fc6_out, fc7_out)


def solution(mesh):
    return jax.shard_map(
        per_device,
        mesh=mesh,
        in_specs=(
            P(("dp", "head"), None, None),
            P("section", None, None),
            P("section", None, None),
            P(None, None, "section"),
            P("section", None, None),
            P(),
            P(None, ("dp", "head"), None),
            P(None, None, None, ("dp", "head"), None),
            P(("dp", "head"), None, None),
            P(("dp", "head"), None, None, None),
        ),
        out_specs=(
            P("section", ("dp", "head"), None),
            P("section", ("dp", "head"), None),
            P(None, None, "section"),
            P("section", None, ("dp", "head")),
            P(None, ("dp", "head")),
        ),
        check_vma=False,
    )
```
